128 devices in a mesh: mem: 32 (over z, y, core), tp: 4 (over x).
Axes of the slice: x: 4, y: 4, z: 4, core: 2. Of those that a mesh axis runs over, the one named last changes fastest.
Arguments:
- hidden_states: bfloat16 [8192, 2048], P('mem', 'tp'), may hold values from -6 to 6
- entry_rescale_coefficients: bfloat16 [2048], replicated, may hold values from 0.099609375 to 1.8984375
- probe_projection_matrix: bfloat16 [2048, 2048], P(None, 'tp'), may hold values from -0.125 to 0.125
- address_projection_matrix: bfloat16 [2048, 2048], P(None, 'tp'), may hold values from -0.125 to 0.125
- content_projection_matrix: bfloat16 [2048, 2048], P(None, 'tp'), may hold values from -0.125 to 0.125
- final_projection_matrix: bfloat16 [2048, 2048], P('tp'), may hold values from -0.125 to 0.125
- archive_address_vectors: bfloat16 [131072, 2048], P('mem', 'tp'), may hold values from -6 to 6
- archive_content_vectors: bfloat16 [131072, 2048], P('mem', 'tp'), may hold values from -6 to 6
- reader_sharpness: float32 [16], P('tp'), may hold values from 16 to 48
- reader_mixing_bias: float32 [16], P('tp'), may hold values from 0.5 to 2
- retrieval_assignments: int32 [64, 8], replicated, may hold values from 0 to 255, as said below
- document_labels: int32 [8192], replicated, may hold values from 0 to 63, never falling along the last dimension, each value on 1 to 512 neighbouring positions
Outputs:
- layer_out: bfloat16 [8192, 2048], P(('mem', 'tp'))
The draws below stay inside these ranges and needn't reach their ends.
Inputs may be any that keep to these rules, and one draw needn't show every extreme that they name: `retrieval_assignments`: the 8 ids of each query block differ. Block m is held by index m // 8 of mem. Of the 16 ids of the query blocks on one index of mem, at most 1 name blocks held by one index of mem, and in every draw some index of mem is named exactly 1 times by the query blocks of every index.
All inputs are finite; a program needn't handle non-finite values.
Results may differ from the reference program's by a relative error of at most 0.015.
Values may be sent and summed in bfloat16 or wider, within the bound.
No kernel may reach another device: no remote copies, remote signals or barrier semaphores. Data moves between devices by JAX's collectives and lax.ppermute only.
A program may use at most 128 MiB of HBM per device.

```python
import math
import jax
import jax.numpy as jnp
import numpy as np
from jax import lax

D = 2048
PARALLEL_READERS = 16
QB = 128
TOPK = 8
MB = 512
MBD = 8
LOCAL = 256
TOKENS = 8192
QBD = 2
QBLOCKS = 64
MEMBLOCKS = 256
MEMTOK = 131072
CAP = 1
N_MEM = 32


def draw_retrieval_assignments(key, part):
    key = jax.random.fold_in(key, 17)
    favour_key, source_key = jax.random.split(key)
    pool_size = N_MEM * CAP
    pair_count = QBD * TOPK
    favoured = jax.random.randint(favour_key, (), 0, N_MEM)

    def one_source(source_seed):
        score_key, order_key, offset_key = jax.random.split(source_seed, 3)
        pool_owner = jnp.repeat(jnp.arange(N_MEM, dtype=jnp.int32), CAP)
        scores = jax.random.randint(score_key, (pool_size,), 0, 1 << 20)
        scores = jnp.where(pool_owner == favoured, -1, scores)
        scores = scores * pool_size + jnp.arange(pool_size, dtype=jnp.int32)
        chosen = pool_owner[jnp.argsort(scores)[:pair_count]]
        chosen = chosen[jax.random.permutation(order_key, pair_count)]
        offsets = jax.random.randint(offset_key, (N_MEM,), 0, MBD)
        same_owner = chosen[:, None] == chosen[None, :]
        earlier = jnp.sum(jnp.tril(same_owner, -1).astype(jnp.int32), axis=1)
        local_index = (offsets[chosen] + earlier) % MBD
        return chosen * MBD + local_index
    result = jax.vmap(one_source)(jax.random.split(source_key, N_MEM))
    return result.reshape(QBLOCKS, TOPK).astype(jnp.int32)


def level_of(rng, extent, cuts, smallest, high):
    gain = 1.0
    for axis_at, shards_of in cuts:
        steps = jax.random.uniform(jax.random.fold_in(jax.random.fold_in(rng, 6), axis_at), (shards_of,), jnp.float32, smallest / len(cuts), high / len(cuts))
        gain = gain * jnp.repeat(jnp.exp(steps), extent[axis_at] // shards_of).reshape((-1,) + (1,) * (len(extent) - 1 - axis_at))
    return gain


def length_profile(count, total, bound, slope):
    loads = [(1 << 20) // math.isqrt(rank ** slope) + 1 for rank in range(2, count + 1)]
    rest, counts = total - bound - (count - 1), [1] * (count - 1)
    while rest > 0:
        candidates = [i for i in range(count - 1) if counts[i] < bound]
        whole, remaining = sum([loads[i] for i in candidates]), rest
        for i in candidates:
            extra = min(bound - counts[i], max(1, remaining * loads[i] // whole), rest)
            counts[i] = counts[i] + extra
            rest = rest - extra
    return np.array([bound] + counts)


def ragged(key, amount, total, limit, skew):
    if amount == 2:
        one = jax.random.randint(key, (), max(1, total - limit), min(limit, total - 1) + 1)
        return jnp.stack([one, total - one])
    lengths = jnp.asarray(length_profile(amount, total, limit, skew), jnp.int32)
    pairs = (amount - 1) // 2
    giver, taker = lengths[1:1 + 2 * pairs:2], lengths[2:2 + 2 * pairs:2]
    room = jnp.minimum(giver - 1, limit - taker)
    shifted = jax.random.randint(jax.random.fold_in(key, 1), (pairs,), 0, 1 << 20) % (room + 1)
    lengths = lengths.at[1:1 + 2 * pairs:2].set(giver - shifted).at[2:2 + 2 * pairs:2].set(taker + shifted)
    return lengths[jax.random.permutation(jax.random.fold_in(key, 2), amount)]


def bell_draw(own_key, shape, width, limit, shards=(), kind=jnp.bfloat16):
    values = jax.random.normal(own_key, shape, jnp.float32) * width
    if len(shards) > 0:
        values = level_of(own_key, shape, shards, -0.22, 0.18) * values
    return jnp.clip(values, min=-limit, max=limit).astype(kind)


def setup_inputs(seed: int = 0) -> dict:
    key_of = jax.random.split(jax.random.key(seed), 13)
    return {
        "hidden_states": bell_draw(key_of[0], (TOKENS, D), 1.0, 6.0, ((0, 32), (1, 4))),
        "entry_rescale_coefficients": jnp.clip(1.0 + 0.18 * jax.random.normal(key_of[1], (D,), jnp.float32), 0.099609375, 1.8984375).astype(jnp.bfloat16),
        "probe_projection_matrix": bell_draw(key_of[2], (D, D), D ** -0.5, 0.125, ((1, 4),)),
        "address_projection_matrix": bell_draw(key_of[3], (D, D), D ** -0.5, 0.125, ((1, 4),)),
        "content_projection_matrix": bell_draw(key_of[4], (D, D), D ** -0.5, 0.125, ((1, 4),)),
        "final_projection_matrix": bell_draw(key_of[5], (D, D), D ** -0.5, 0.125, ((0, 4),)),
        "archive_address_vectors": bell_draw(key_of[6], (MEMTOK, D), 1.0, 6.0, ((0, 32), (1, 4))),
        "archive_content_vectors": bell_draw(key_of[7], (MEMTOK, D), 1.0, 6.0, ((0, 32), (1, 4))),
        "reader_sharpness": jnp.clip(jnp.exp(math.log(48.0) - 1.0986123 * jax.random.uniform(key_of[8], (PARALLEL_READERS,), jnp.float32) ** level_of(key_of[8], (PARALLEL_READERS,), ((0, 4),), -0.2, 0.2)), 16.0, 48.0),
        "reader_mixing_bias": jnp.clip(0.5 + 1.5 * jax.random.uniform(key_of[9], (PARALLEL_READERS,), jnp.float32) ** level_of(key_of[9], (PARALLEL_READERS,), ((0, 4),), -0.2, 0.2), 0.5, 2.0),
        "retrieval_assignments": draw_retrieval_assignments(jax.random.fold_in(key_of[12], 71), 0),
        "document_labels": jnp.searchsorted(jnp.cumsum(ragged(key_of[11], TOKENS // (LOCAL // 2), TOKENS, 2 * LOCAL, 2)), jnp.arange(TOKENS), side="right").astype(jnp.int32),
    }


def rounded(values):
    return lax.optimization_barrier(values.astype(jnp.bfloat16)).astype(jnp.float32)

def unit_heads(matrix, reader_number):
    row_count = matrix.shape[0]
    shaped = matrix.astype(jnp.float32).reshape(row_count, reader_number, -1)
    dot_product_multiplier = lax.rsqrt(lax.optimization_barrier(jnp.mean(shaped * shaped, axis=-1, keepdims=True)) + 1e-06)
    return (shaped * dot_product_multiplier).astype(jnp.bfloat16)

def reference(hidden_states, entry_rescale_coefficients, probe_projection_matrix, address_projection_matrix, content_projection_matrix, final_projection_matrix, archive_address_vectors, archive_content_vectors, reader_sharpness, reader_mixing_bias, retrieval_assignments, document_labels):
    reader_dimension = D // PARALLEL_READERS
    widened = hidden_states.astype(jnp.float32)
    normed = (widened * lax.rsqrt(lax.optimization_barrier(jnp.mean(widened * widened, axis=-1, keepdims=True)) + 1e-05) * entry_rescale_coefficients.astype(jnp.float32)).astype(jnp.bfloat16)
    queries = unit_heads(jnp.dot(normed, probe_projection_matrix, preferred_element_type=jnp.float32), PARALLEL_READERS)
    local_keys = unit_heads(jnp.dot(normed, address_projection_matrix, preferred_element_type=jnp.float32), PARALLEL_READERS)
    local_values = jnp.dot(normed, content_projection_matrix, preferred_element_type=jnp.float32).astype(jnp.bfloat16).reshape(TOKENS, PARALLEL_READERS, reader_dimension)
    dot_product_multiplier = reader_sharpness.astype(jnp.float32) / reader_dimension
    padded_keys = jnp.concatenate([jnp.zeros((LOCAL, PARALLEL_READERS, reader_dimension), jnp.bfloat16), local_keys], axis=0)
    padded_values = jnp.concatenate([jnp.zeros((LOCAL, PARALLEL_READERS, reader_dimension), jnp.bfloat16), local_values], axis=0)
    padded_segments = jnp.concatenate([jnp.full((LOCAL,), -1, jnp.int32), document_labels.astype(jnp.int32)], axis=0)
    query_place = jnp.arange(LOCAL, dtype=jnp.int32) + LOCAL
    key_place = jnp.arange(2 * LOCAL, dtype=jnp.int32)

    def local_block(index):
        begin = (index * LOCAL).astype(jnp.int32)
        query_rows = lax.dynamic_slice_in_dim(queries, begin, LOCAL, 0).astype(jnp.float32)
        key_rows = lax.dynamic_slice_in_dim(padded_keys, begin, 2 * LOCAL, 0).astype(jnp.float32)
        value_rows = lax.dynamic_slice_in_dim(padded_values, begin, 2 * LOCAL, 0).astype(jnp.float32)
        query_segment = lax.dynamic_slice_in_dim(document_labels.astype(jnp.int32), begin, LOCAL, 0)
        key_segment = lax.dynamic_slice_in_dim(padded_segments, begin, 2 * LOCAL, 0)
        allowed = (key_place[None, :] <= query_place[:, None]) & (query_place[:, None] - key_place[None, :] < LOCAL) & (query_segment[:, None] == key_segment[None, :])
        scores = jnp.einsum('qhd,khd->hqk', query_rows, key_rows) * dot_product_multiplier[:, None, None]
        weights = jnp.exp(scores) * allowed[None].astype(jnp.float32)
        totals = lax.optimization_barrier(jnp.sum(weights, axis=-1))
        numer = jnp.einsum('hqk,khd->qhd', rounded(weights), value_rows)
        return numer / jnp.transpose(totals)[:, :, None]
    local_out = lax.map(local_block, jnp.arange(TOKENS // LOCAL, dtype=jnp.int32)).reshape(TOKENS, PARALLEL_READERS, reader_dimension)
    memory_keys = unit_heads(archive_address_vectors, PARALLEL_READERS).reshape(MEMBLOCKS, MB, PARALLEL_READERS, reader_dimension)
    memory_values = archive_content_vectors.reshape(MEMBLOCKS, MB, PARALLEL_READERS, reader_dimension)
    query_blocks = queries.reshape(QBLOCKS, QB, PARALLEL_READERS, reader_dimension)

    def memory_block(item):
        query_rows, block_ids = item
        key_rows = jnp.take(memory_keys, block_ids.astype(jnp.int32), axis=0).astype(jnp.float32)
        value_rows = jnp.take(memory_values, block_ids.astype(jnp.int32), axis=0).astype(jnp.float32)
        scores = jnp.einsum('qhd,jmhd->jhqm', query_rows.astype(jnp.float32), key_rows) * dot_product_multiplier[None, :, None, None]
        weights = jnp.exp(scores)
        totals = lax.optimization_barrier(jnp.sum(weights, axis=-1))
        numer = jnp.einsum('jhqm,jmhd->jqhd', rounded(weights), value_rows)
        part_totals = jnp.transpose(totals, (0, 2, 1))
        part_out = rounded(numer / part_totals[..., None])
        part_den = rounded(part_totals)
        return jnp.einsum('jqh,jqhd->qhd', part_den, part_out) / lax.optimization_barrier(jnp.sum(part_den, axis=0))[..., None]
    memory_out = lax.map(memory_block, (query_blocks, retrieval_assignments)).reshape(TOKENS, PARALLEL_READERS, reader_dimension)
    gate_value = jax.nn.sigmoid(reader_mixing_bias.astype(jnp.float32))[None, :, None]
    mixed = (gate_value * memory_out + (1.0 - gate_value) * local_out).astype(jnp.bfloat16).reshape(TOKENS, D)
    return jnp.dot(mixed, final_projection_matrix, preferred_element_type=jnp.float32).astype(jnp.bfloat16)
```

```python
import functools

import jax
import jax.numpy as jnp
from jax import lax
from jax.experimental import pallas as pl
from jax.experimental.pallas import tpu as pltpu
from jax.sharding import PartitionSpec as P

QB = 128
MB = 512
LOCAL = 256
HD = 128
LOG2E = 1.4426950408889634
NT = (((1,), (1,)), ((), ()))
VMEM = pl.BlockSpec(memory_space=pltpu.VMEM)
SMEM = pl.BlockSpec(memory_space=pltpu.SMEM)
F32 = jnp.float32
BF16 = jnp.bfloat16


def params(mib):
    return pltpu.CompilerParams(vmem_limit_bytes=mib * 2**20)


def cost(flops, nbytes, trans=0):
    return pl.CostEstimate(flops=flops, bytes_accessed=nbytes, transcendentals=trans)


def unit_into(ref, rows, value):
    for h in range(value.shape[1] // HD):
        part = value[:, h * HD : (h + 1) * HD]
        scale = lax.rsqrt(jnp.mean(part * part, axis=-1, keepdims=True) + 1e-06)
        ref[rows, h * HD : (h + 1) * HD] = (part * scale).astype(BF16)


def query_kernel(order, x0, x1, x2, x3, gain, weight, normed, queries):
    pieces = [x[...].astype(F32) for x in (x0, x1, x2, x3)]
    total = sum(jnp.sum(p * p, axis=-1, keepdims=True) for p in pieces)
    scale = lax.rsqrt(total / (4 * pieces[0].shape[1]) + 1e-05)
    result = None
    for p, piece in enumerate(pieces):
        value = (piece * scale * gain[order[p]].astype(F32)).astype(BF16)
        normed[p] = value
        term = jnp.dot(value, weight[order[p]], preferred_element_type=F32)
        result = term if result is None else result + term
    unit_into(queries, slice(None), result)


def kv_kernel(order, normed, key_weight, value_weight, kv):
    for side, weight in enumerate((key_weight, value_weight)):
        result = None
        for p in range(4):
            term = jnp.dot(normed[p], weight[order[p]], preferred_element_type=F32)
            result = term if result is None else result + term
        if side == 0:
            unit_into(kv.at[0], slice(None), result)
        else:
            kv[1] = result.astype(BF16)


def key_unit_kernel(raw, keys):
    unit_into(keys, slice(None), raw[...].astype(F32))


def local_kernel(sharp, seg_own, seg_keys, queries, kv, before, out):
    rows = queries.shape[0]
    place = lax.broadcasted_iota(jnp.int32, (rows, rows), 0)
    other = lax.broadcasted_iota(jnp.int32, (rows, rows), 1)
    same_before = seg_own[...] == seg_keys[:, :rows]
    same_own = seg_own[...] == seg_keys[:, rows:]
    allow_before = (other > place) & same_before
    allow_own = (other <= place) & same_own
    for h in range(queries.shape[1] // HD):
        cols = slice(h * HD, (h + 1) * HD)
        scale = sharp[h] * (LOG2E / HD)
        q = queries[:, cols]
        numer = None
        total = None
        for keep, src in ((allow_before, before), (allow_own, kv)):
            s = lax.dot_general(q, src[0, :, cols], NT, preferred_element_type=F32)
            w = jnp.where(keep, jnp.exp2(s * scale), 0.0)
            t = jnp.sum(w, axis=-1, keepdims=True)
            n = jnp.dot(w.astype(BF16), src[1, :, cols], preferred_element_type=F32)
            numer = n if numer is None else numer + n
            total = t if total is None else total + t
        out[:, cols] = numer / total


def memory_kernel(meta, sharp, q1, q2, k_own, v_own, k_sib, v_sib, o1, o2):
    i = pl.program_id(0)
    eye = lax.broadcasted_iota(jnp.int32, (QB, QB), 0) == lax.broadcasted_iota(
        jnp.int32, (QB, QB), 1
    )
    tile_row = lax.broadcasted_iota(jnp.int32, (16, HD), 0)

    def work(q_ref, o_ref):
        o_ref[...] = jnp.zeros_like(o_ref)

        def slot(j, k_ref, v_ref):
            half = meta[i, 4 + j]
            rows = pl.ds(pl.multiple_of(half * QB, QB), QB)
            for h in range(q_ref.shape[2] // HD):
                cols = slice(h * HD, (h + 1) * HD)
                scale = sharp[h] * (LOG2E / HD)
                s = lax.dot_general(
                    q_ref[0, rows, cols], k_ref[:, cols], NT, preferred_element_type=F32
                )
                w = jnp.exp2(s * scale)
                den = jnp.sum(w, axis=-1, keepdims=True)
                num = jnp.dot(w.astype(BF16), v_ref[:, cols], preferred_element_type=F32)
                line = jnp.sum(jnp.where(eye, den, 0.0), axis=0, keepdims=True)
                dens = jnp.where(tile_row == half, line, 0.0)
                if j == 1:
                    num = num + o_ref[0, rows, cols].astype(F32)
                    dens = dens + o_ref[0, 2 * QB :, cols].astype(F32)
                o_ref[0, rows, cols] = num.astype(BF16)
                o_ref[0, 2 * QB :, cols] = dens.astype(BF16)

        pl.when(meta[i, 2] > 0)(lambda: slot(0, k_own, v_own))
        pl.when(meta[i, 3] > 0)(lambda: slot(1, k_sib, v_sib))

    pl.when(i < 2)(lambda: work(q1, o1))
    pl.when(i >= 2)(lambda: work(q2, o2))


def memory_attention(meta, sharp, q1, q2, k_own, v_own, k_sib, v_sib):
    width = q1.shape[2]
    first = lambda i, meta: (jnp.minimum(i, 1), 0, 0)
    second = lambda i, meta: (jnp.maximum(i - 2, 0), 0, 0)
    own = lambda i, meta: (meta[i, 0], 0)
    sib = lambda i, meta: (meta[i, 1], 0)
    block = lambda m: pl.BlockSpec((MB, width), m)
    part = lambda m: pl.BlockSpec((1, 2 * QB, width), m)
    done = lambda m: pl.BlockSpec((1, 2 * QB + 16, width), m)
    shape = jax.ShapeDtypeStruct((2, 2 * QB + 16, width), BF16)
    return pl.pallas_call(
        memory_kernel,
        grid_spec=pltpu.PrefetchScalarGridSpec(
            num_scalar_prefetch=1,
            grid=(4,),
            in_specs=[
                SMEM,
                part(first),
                part(second),
                block(own),
                block(own),
                block(sib),
                block(sib),
            ],
            out_specs=[done(first), done(second)],
        ),
        out_shape=[shape, shape],
        compiler_params=params(24),
        cost_estimate=cost(8 * 134_000_000, 8 * 2**20, 8 * QB * MB * 4),
        name="memory_attention",
    )(meta, sharp, q1, q2, k_own, v_own, k_sib, v_sib)


def output_kernel(order, bias, w, x1, x2, x3, local, weight, c0, c1, c2, c3, mixed):
    total = [a[0].astype(F32) if a.ndim == 3 else a[...].astype(F32) for a in (w, x1, x2, x3)]
    total = total[0] + total[1] + total[2] + total[3]
    dens = total[2 * QB :, :]
    for h in range(total.shape[1] // HD):
        cols = slice(h * HD, (h + 1) * HD)
        gate = jax.nn.sigmoid(jnp.full((1, HD), bias[h], F32))
        turned = jnp.transpose(
            jnp.concatenate([dens[:, cols], jnp.zeros((HD - 16, HD), F32)], axis=0)
        )
        for b in range(2):
            rows = slice(b * QB, (b + 1) * QB)
            mem = total[rows, cols] / turned[:, b : b + 1]
            mixed[rows, cols] = (gate * mem + (1.0 - gate) * local[rows, cols]).astype(BF16)
    for j, c in enumerate((c0, c1, c2, c3)):
        rows = pl.ds(pl.multiple_of(order[j] * 64, 64), 64)
        c[...] = jnp.dot(mixed[rows, :], weight[...], preferred_element_type=F32).astype(c.dtype)


def mem_pairs(move):
    out = []
    for z in range(4):
        for y in range(4):
            for c in range(2):
                tz, ty, tc = move(z, y, c)
                out.append((z * 8 + y * 2 + c, (tz % 4) * 8 + (ty % 4) * 2 + tc))
    return out


def first_axis(value, by):
    pairs = mem_pairs(lambda z, y, c: (z + by, y, c) if c == 0 else (z, y + by, c))
    return lax.ppermute(value, "mem", pairs)


def second_axis(value, by):
    pairs = mem_pairs(lambda z, y, c: (z, y + by, c) if c == 0 else (z + by, y, c))
    return lax.ppermute(value, "mem", pairs)


def other_core(value):
    return lax.ppermute(value, "mem", mem_pairs(lambda z, y, c: (z, y, 1 - c)))


def along_tp(value, by):
    return lax.ppermute(value, "tp", [(i, (i + by) % 4) for i in range(4)])


def make_meta(assign, index, blocks_here):
    z, y, c = index // 8, (index // 2) % 4, index % 2
    shifts = jnp.array([0, -1, 1, 2], jnp.int32)
    second = jnp.array([0, -1, 1, 2], jnp.int32)[:, None]
    first = shifts[None, :]
    sz = jnp.where(c == 0, z + first, z + second) % 4
    sy = jnp.where(c == 0, y + second, y + first) % 4
    source = sz * 8 + sy * 2 + c
    ids = jnp.take(assign.reshape(-1, 16), source.reshape(-1), axis=0)
    holder = jnp.stack([index, index + 1 - 2 * c])
    hit = (ids // blocks_here)[:, None, :] == holder[None, :, None]
    here = jnp.any(hit, axis=-1).astype(jnp.int32).reshape(4, 4, 2)
    block = jnp.sum(jnp.where(hit, (ids % blocks_here)[:, None, :], 0), axis=-1).reshape(4, 4, 2)
    place = jnp.arange(16, dtype=jnp.int32)[None, None, :] // 8
    half = jnp.sum(jnp.where(hit, place, 0), axis=-1).reshape(4, 4, 2)
    fetch = [block[:, 0]]
    for i in range(1, 4):
        fetch.append(jnp.where(here[:, i] > 0, block[:, i], fetch[-1]))
    return jnp.concatenate([jnp.stack(fetch, axis=1), here, half], axis=-1)


def add(a, b):
    return (a.astype(F32) + b.astype(F32)).astype(BF16)


def add3(a, b, c):
    return (a.astype(F32) + b.astype(F32) + c.astype(F32)).astype(BF16)


def body(
    hidden_states,
    entry_rescale_coefficients,
    probe_projection_matrix,
    address_projection_matrix,
    content_projection_matrix,
    final_projection_matrix,
    archive_address_vectors,
    archive_content_vectors,
    reader_sharpness,
    reader_mixing_bias,
    retrieval_assignments,
    document_labels,
):
    rows, piece = hidden_states.shape
    width = probe_projection_matrix.shape[1]
    index = lax.axis_index("mem")
    me = lax.axis_index("tp")
    order = (me + jnp.array([0, -1, 1, 2], jnp.int32)) % 4

    x1 = along_tp(hidden_states, 1)
    x2 = along_tp(hidden_states, -1)
    x3 = along_tp(hidden_states, 2)

    v_own = archive_content_vectors
    v_sib = other_core(v_own)
    k_own = pl.pallas_call(
        key_unit_kernel,
        grid=(8,),
        in_specs=[pl.BlockSpec((MB, width), lambda i: (i, 0))],
        out_specs=pl.BlockSpec((MB, width), lambda i: (i, 0)),
        out_shape=jax.ShapeDtypeStruct(archive_address_vectors.shape, BF16),
        compiler_params=params(16),
        cost_estimate=cost(10 * 2**20, 8 * 2**20),
        name="key_unit",
    )(archive_address_vectors)
    k_sib = other_core(k_own)

    meta = make_meta(retrieval_assignments, index, archive_address_vectors.shape[0] // MB)

    normed, queries = pl.pallas_call(
        query_kernel,
        in_specs=[SMEM] + [VMEM] * 6,
        out_specs=[VMEM, VMEM],
        out_shape=[
            jax.ShapeDtypeStruct((4, rows, piece), BF16),
            jax.ShapeDtypeStruct((rows, width), BF16),
        ],
        compiler_params=params(24),
        cost_estimate=cost(2 * rows * 4 * piece * width, 4 * 2**20),
        name="norm_query",
    )(
        order,
        hidden_states,
        x1,
        x2,
        x3,
        entry_rescale_coefficients.reshape(4, 1, piece),
        probe_projection_matrix.reshape(4, piece, width),
    )

    a1 = first_axis(queries, 1)
    a2 = first_axis(queries, -1)
    a3 = first_axis(queries, 2)
    kv = pl.pallas_call(
        kv_kernel,
        in_specs=[SMEM] + [VMEM] * 3,
        out_specs=VMEM,
        out_shape=jax.ShapeDtypeStruct((2, rows, width), BF16),
        compiler_params=params(24),
        cost_estimate=cost(4 * rows * 4 * piece * width, 6 * 2**20),
        name="local_kv",
    )(
        order,
        normed,
        address_projection_matrix.reshape(4, piece, width),
        content_projection_matrix.reshape(4, piece, width),
    )
    m1 = jnp.stack([queries, a1])
    m2 = jnp.stack([a2, a3])
    b1p = second_axis(m1, 1)
    b1m = second_axis(m1, -1)
    b2p = second_axis(m2, 1)
    b2m = second_axis(m2, -1)
    c1 = second_axis(b1p, 1)
    c2 = second_axis(b2m, -1)

    count = lax.axis_size("mem")
    before = lax.ppermute(kv, "mem", [(i, i + 1) for i in range(count - 1)])
    first_row = index * rows
    seg_own = lax.dynamic_slice_in_dim(document_labels, first_row, rows, 0)
    seg_before = lax.dynamic_slice_in_dim(
        document_labels, jnp.maximum(first_row - rows, 0), rows, 0
    )
    seg_before = jnp.where(index > 0, seg_before, -1)
    seg_keys = jnp.concatenate([seg_before, seg_own], axis=0)
    local_out = pl.pallas_call(
        local_kernel,
        in_specs=[SMEM] + [VMEM] * 5,
        out_specs=VMEM,
        out_shape=jax.ShapeDtypeStruct((rows, width), F32),
        compiler_params=params(24),
        cost_estimate=cost(2**28, 2 * 2**20, 2**19),
        name="local_attention",
    )(reader_sharpness, seg_own[:, None], seg_keys[None, :], queries, kv, before)

    attend = lambda g, q1, q2: memory_attention(
        meta[g], reader_sharpness, q1, q2, k_own, v_own, k_sib, v_sib
    )
    z1, z2 = attend(0, m1, m2)
    n1, n2 = attend(1, b1p, b2p)
    p1, p2 = attend(2, b1m, b2m)
    f1, f2 = attend(3, c1, c2)

    t1 = second_axis(f1, 1)
    t2 = second_axis(f2, -1)
    u2 = second_axis(p2, 1)
    v1 = second_axis(n1, -1)
    u1 = second_axis(add(p1, t1), 1)
    v2 = second_axis(add(n2, t2), -1)
    w1 = add3(z1, u1, v1)
    w2 = add3(z2, u2, v2)
    r1 = first_axis(w1[1], -1)
    r2 = first_axis(w2[0], 1)
    r3 = first_axis(w2[1], 2)

    chunk = jax.ShapeDtypeStruct((rows // 4, 4 * piece), BF16)
    c0, d1, d2, d3 = pl.pallas_call(
        output_kernel,
        in_specs=[SMEM, SMEM] + [VMEM] * 6,
        out_specs=[VMEM] * 4,
        out_shape=[chunk] * 4,
        scratch_shapes=[pltpu.VMEM((rows, width), BF16)],
        compiler_params=params(32),
        cost_estimate=cost(2 * rows * width * 4 * piece, 5 * 2**20),
        name="merge_output",
    )(order, reader_mixing_bias, w1[0], r1, r2, r3, local_out, final_projection_matrix)
    e1 = along_tp(d1, -1)
    e2 = along_tp(d2, 1)
    e3 = along_tp(d3, 2)
    total = c0.astype(F32) + e1.astype(F32) + e2.astype(F32) + e3.astype(F32)
    return total.astype(BF16)


def solution(mesh):
    placed = (
        P("mem", "tp"),
        P(),
        P(None, "tp"),
        P(None, "tp"),
        P(None, "tp"),
        P("tp", None),
        P("mem", "tp"),
        P("mem", "tp"),
        P("tp"),
        P("tp"),
        P(),
        P(),
    )
    return jax.shard_map(
        body, mesh=mesh, in_specs=placed, out_specs=P(("mem", "tp"), None), check_vma=False
    )
```

```python
import functools

import jax
import jax.numpy as jnp
from jax import lax
from jax.experimental import pallas as pl
from jax.experimental.pallas import tpu as pltpu
from jax.sharding import PartitionSpec as P

QB = 128
MB = 512
LOCAL = 256
HD = 128
LOG2E = 1.4426950408889634
NT = (((1,), (1,)), ((), ()))
VMEM = pl.BlockSpec(memory_space=pltpu.VMEM)
SMEM = pl.BlockSpec(memory_space=pltpu.SMEM)
F32 = jnp.float32
BF16 = jnp.bfloat16


def params(mib=40):
    return pltpu.CompilerParams(vmem_limit_bytes=mib * 2**20)


def cost(us):
    return pl.CostEstimate(flops=1, bytes_accessed=int(us * 3.69e6), transcendentals=0)


def unit_into(ref, rows, value):
    for h in range(value.shape[1] // HD):
        part = value[:, h * HD : (h + 1) * HD]
        scale = lax.rsqrt(jnp.mean(part * part, axis=-1, keepdims=True) + 1e-06)
        ref[rows, h * HD : (h + 1) * HD] = (part * scale).astype(BF16)


def norm_pieces(order, pieces, gain):
    pieces = [x[...].astype(F32) for x in pieces]
    total = sum(jnp.sum(p * p, axis=-1, keepdims=True) for p in pieces)
    scale = lax.rsqrt(total / (4 * pieces[0].shape[1]) + 1e-05)
    return [
        (piece * scale * gain[order[p]].astype(F32)).astype(BF16)
        for p, piece in enumerate(pieces)
    ]


def project(order, normed, weight):
    result = None
    for p, value in enumerate(normed):
        term = jnp.dot(value, weight[order[p]], preferred_element_type=F32)
        result = term if result is None else result + term
    return result


def query_kernel(order, x0, x1, x2, x3, gain, weight, queries, x, w, x_sem, w_sem):
    loads = [
        pltpu.make_async_copy(part, x.at[p], x_sem.at[p]) for p, part in enumerate((x0, x1, x2, x3))
    ]
    fetches = [
        pltpu.make_async_copy(weight.at[order[p]], w.at[p], w_sem.at[p]) for p in range(4)
    ]
    for copy in loads + fetches:
        copy.start()
    for copy in loads:
        copy.wait()
    normed = norm_pieces(order, [x.at[p] for p in range(4)], gain)
    result = None
    for p, value in enumerate(normed):
        fetches[p].wait()
        term = jnp.dot(value, w[p], preferred_element_type=F32)
        result = term if result is None else result + term
    unit_into(queries, slice(None), result)


def kv_kernel(order, x0, x1, x2, x3, gain, key_weight, value_weight, kv):
    normed = norm_pieces(order, (x0, x1, x2, x3), gain)
    unit_into(kv.at[0], slice(None), project(order, normed, key_weight))
    kv[1] = project(order, normed, value_weight).astype(BF16)


def key_unit_kernel(raw, keys, x, sem):
    blocks = x.shape[0]
    loads = [
        pltpu.make_async_copy(raw.at[pl.ds(b * MB, MB)], x.at[b], sem.at[b]) for b in range(blocks)
    ]
    for load in loads:
        load.start()
    wide = 2 * HD
    place = lambda d: lax.broadcasted_iota(jnp.int32, (wide, wide), d) // HD
    ones = (place(0) == place(1)).astype(BF16)

    def step(b, _):
        pltpu.make_async_copy(raw.at[pl.ds(0, MB)], x.at[b], sem.at[b]).wait()
        rows = pl.ds(pl.multiple_of(b * MB, MB), MB)
        for c in range(x.shape[2] // wide):
            cols = slice(c * wide, (c + 1) * wide)
            part = x[b, :, cols].astype(F32)
            total = jnp.dot((part * part).astype(BF16), ones, preferred_element_type=F32)
            keys[rows, cols] = (part * lax.rsqrt(total * (1 / HD) + 1e-06)).astype(BF16)
        return 0

    lax.fori_loop(0, blocks, step, 0)


def key_unit(raw):
    blocks = raw.shape[0] // MB
    return pl.pallas_call(
        key_unit_kernel,
        in_specs=[pl.BlockSpec(memory_space=pl.ANY)],
        out_specs=VMEM,
        out_shape=jax.ShapeDtypeStruct(raw.shape, BF16),
        scratch_shapes=[
            pltpu.VMEM((blocks, MB, raw.shape[1]), BF16),
            pltpu.SemaphoreType.DMA((blocks,)),
        ],
        compiler_params=params(),
        cost_estimate=cost(6),
        name="key_unit",
    )(raw)


def local_kernel(index, sharp, labels, queries, kv, before, out):
    rows = queries.shape[0]
    place = lax.broadcasted_iota(jnp.int32, (rows, rows), 0)
    other = lax.broadcasted_iota(jnp.int32, (rows, rows), 1)
    line = lambda r: labels[pl.ds(r, 1), :].astype(F32)
    here = 2 * index[0]
    own = [line(here), line(here + 1)]
    past = [line(jnp.maximum(here - 2, 0)), line(jnp.maximum(here - 1, 0))]
    queried = jnp.concatenate(
        [jnp.transpose(jnp.broadcast_to(o, (QB, QB)))[:, :1] for o in own], axis=0
    )
    same_before = (queried == jnp.concatenate(past, axis=1)) & (index[0] > 0)
    same_own = queried == jnp.concatenate(own, axis=1)
    allow_before = (other > place) & same_before
    allow_own = (other <= place) & same_own
    for h in range(queries.shape[1] // HD):
        cols = slice(h * HD, (h + 1) * HD)
        scale = sharp[h] * (LOG2E / HD)
        q = queries[:, cols]
        numer = None
        total = None
        for keep, src in ((allow_before, before), (allow_own, kv)):
            s = lax.dot_general(q, src[0, :, cols], NT, preferred_element_type=F32)
            w = jnp.where(keep, jnp.exp2(s * scale), 0.0)
            t = jnp.sum(w, axis=-1, keepdims=True)
            n = jnp.dot(w.astype(BF16), src[1, :, cols], preferred_element_type=F32)
            numer = n if numer is None else numer + n
            total = t if total is None else total + t
        out[:, cols] = numer / total


def memory_kernel(first, meta, sharp, *refs):
    n = (len(refs) - 8) // 2
    parts, sources = refs[:n], (refs[n : n + 2], refs[n + 2 : n + 4])
    outs, (q, o, in_sem, out_sem) = refs[n + 4 : 2 * n + 4], refs[2 * n + 4 :]
    heads = q.shape[2] // HD
    loads = [
        pltpu.make_async_copy(parts[i // 2].at[i % 2], q.at[i], in_sem.at[i]) for i in range(2 * n)
    ]
    stores = [
        pltpu.make_async_copy(o.at[i], outs[i // 2].at[i % 2], out_sem.at[i]) for i in range(2 * n)
    ]
    for load in loads:
        load.start()
    eye = lax.broadcasted_iota(jnp.int32, (QB, QB), 0) == lax.broadcasted_iota(
        jnp.int32, (QB, QB), 1
    )
    tile_row = lax.broadcasted_iota(jnp.int32, (16, HD), 0)
    cols = [slice(h * HD, (h + 1) * HD) for h in range(heads)]
    o[...] = jnp.zeros_like(o)
    for load in loads:
        load.wait()

    def group(g, _):
        for j, (k, v) in enumerate(sources):
            base = ((first + g) * 2 + j) * 13

            def step(p, _, j=j, k=k, v=v, base=base):
                i = meta[base + 1 + p * 3] + 4 * g
                half = meta[base + 2 + p * 3]
                b = meta[base + 3 + p * 3]
                rows = pl.ds(pl.multiple_of(half * QB, QB), QB)
                span = pl.ds(pl.multiple_of(b * MB, MB), MB)
                scores = [
                    lax.dot_general(q[i, rows, c], k[span, c], NT, preferred_element_type=F32)
                    for c in cols
                ]
                weights = [jnp.exp2(s * (sharp[h] * (LOG2E / HD))) for h, s in enumerate(scores)]
                numers = [
                    jnp.dot(w.astype(BF16), v[span, c], preferred_element_type=F32)
                    for w, c in zip(weights, cols)
                ]
                lines = [
                    jnp.sum(
                        jnp.where(eye, jnp.sum(w, axis=-1, keepdims=True), 0.0),
                        axis=0,
                        keepdims=True,
                    )
                    for w in weights
                ]
                for num, line, c in zip(numers, lines, cols):
                    den = jnp.where(tile_row == half, line, 0.0)
                    if j == 1:
                        num = num + o[i, rows, c].astype(F32)
                        den = den + o[i, 2 * QB :, c].astype(F32)
                    o[i, rows, c] = num.astype(BF16)
                    o[i, 2 * QB :, c] = den.astype(BF16)
                return 0

            lax.fori_loop(0, meta[base], step, 0)
        return 0

    lax.fori_loop(0, n // 2, group, 0)
    for store in stores:
        store.start()
    for store in stores:
        store.wait()


def memory_attention(first, meta, sharp, parts, resident):
    width = parts[0].shape[2]
    n = len(parts)
    shape = jax.ShapeDtypeStruct((2, 2 * QB + 16, width), BF16)
    far = pl.BlockSpec(memory_space=pl.ANY)
    return pl.pallas_call(
        functools.partial(memory_kernel, first),
        in_specs=[SMEM, SMEM] + [far] * n + [VMEM] * 4,
        out_specs=[far] * n,
        out_shape=[shape] * n,
        scratch_shapes=[
            pltpu.VMEM((2 * n, 2 * QB, width), BF16),
            pltpu.VMEM((2 * n, 2 * QB + 16, width), BF16),
            pltpu.SemaphoreType.DMA((2 * n,)),
            pltpu.SemaphoreType.DMA((2 * n,)),
        ],
        compiler_params=params(),
        cost_estimate=cost(3 * n),
        name="memory_attention",
    )(meta, sharp, *parts, *resident)


def output_kernel(
    order, bias, z, u, v, x1, x2, x3, local, weight, c0, c1, c2, c3, mixed, w, w_sem
):
    fetch = pltpu.make_async_copy(weight, w, w_sem)
    fetch.start()
    total = z[0].astype(F32) + u[0].astype(F32) + v[0].astype(F32)
    total = total + x1[...].astype(F32) + x2[...].astype(F32) + x3[...].astype(F32)
    dens = total[2 * QB :, :]
    for h in range(total.shape[1] // HD):
        cols = slice(h * HD, (h + 1) * HD)
        gate = jax.nn.sigmoid(jnp.full((1, HD), bias[h], F32))
        turned = jnp.transpose(
            jnp.concatenate([dens[:, cols], jnp.zeros((HD - 16, HD), F32)], axis=0)
        )
        for b in range(2):
            rows = slice(b * QB, (b + 1) * QB)
            mem = total[rows, cols] / turned[:, b : b + 1]
            mixed[rows, cols] = (gate * mem + (1.0 - gate) * local[rows, cols]).astype(BF16)
    fetch.wait()
    for j, c in enumerate((c0, c1, c2, c3)):
        n = c.shape[0]
        rows = pl.ds(pl.multiple_of(order[j] * n, n), n)
        c[...] = jnp.dot(mixed[rows, :], w[...], preferred_element_type=F32).astype(c.dtype)


def mem_pairs(move):
    out = []
    for z in range(4):
        for y in range(4):
            for c in range(2):
                tz, ty, tc = move(z, y, c)
                out.append((z * 8 + y * 2 + c, (tz % 4) * 8 + (ty % 4) * 2 + tc))
    return out


def first_axis(value, by):
    pairs = mem_pairs(lambda z, y, c: (z + by, y, c) if c == 0 else (z, y + by, c))
    return lax.ppermute(value, "mem", pairs)


def second_axis(value, by):
    pairs = mem_pairs(lambda z, y, c: (z, y + by, c) if c == 0 else (z + by, y, c))
    return lax.ppermute(value, "mem", pairs)


def other_core(value):
    return lax.ppermute(value, "mem", mem_pairs(lambda z, y, c: (z, y, 1 - c)))


def along_tp(value, by):
    return lax.ppermute(value, "tp", [(i, (i + by) % 4) for i in range(4)])


def make_meta(assign, index, blocks_here):
    z, y, c = index // 8, (index // 2) % 4, index % 2
    shifts = jnp.array([0, -1, 1, 2], jnp.int32)
    second = jnp.array([0, -1, 1, 2], jnp.int32)[:, None]
    first = shifts[None, :]
    sz = jnp.where(c == 0, z + first, z + second) % 4
    sy = jnp.where(c == 0, y + second, y + first) % 4
    source = sz * 8 + sy * 2 + c
    ids = jnp.take(assign.reshape(-1, 16), source.reshape(-1), axis=0)
    holder = jnp.stack([index, index + 1 - 2 * c])
    hit = (ids // blocks_here)[:, None, :] == holder[None, :, None]
    here = jnp.any(hit, axis=-1).astype(jnp.int32).reshape(4, 4, 2)
    block = jnp.sum(jnp.where(hit, (ids % blocks_here)[:, None, :], 0), axis=-1).reshape(4, 4, 2)
    place = jnp.arange(16, dtype=jnp.int32)[None, None, :] // 8
    half = jnp.sum(jnp.where(hit, place, 0), axis=-1).reshape(4, 4, 2)
    slot = jnp.arange(4, dtype=jnp.int32)
    earlier = slot[:, None] > slot[None, :]
    rank = jnp.sum(jnp.where(earlier[None, :, :, None], here[:, None], 0), axis=2)
    chosen = (here[..., None] > 0) & (rank[..., None] == slot)
    fields = jnp.stack([jnp.broadcast_to(slot[None, :, None], here.shape), half, block], axis=-1)
    table = jnp.sum(jnp.where(chosen[..., None], fields[:, :, :, None, :], 0), axis=1)
    count = jnp.sum(here, axis=1)[..., None]
    return jnp.concatenate([count, table.reshape(4, 2, 12)], axis=-1).reshape(-1)


def add(a, b):
    return (a.astype(F32) + b.astype(F32)).astype(BF16)


def add3(a, b, c):
    return (a.astype(F32) + b.astype(F32) + c.astype(F32)).astype(BF16)


def ordered(first, *later):
    return lax.optimization_barrier((first,) + later)[1:]


FAR = pl.BlockSpec(memory_space=pl.ANY)


def call(us, kernel, name, scalars, arrays, shapes, far=(), scratch=()):
    whole = lambda a: pl.BlockSpec(a.shape, lambda i, n=len(a.shape): (0,) * n)
    specs = [SMEM] * len(scalars)
    values = list(scalars)
    for n, a in enumerate(arrays):
        if isinstance(a, tuple):
            a = a[0]
            specs.append(pl.BlockSpec((1,) + a.shape[1:], lambda i, n=a.ndim: (0,) * n))
        else:
            specs.append(FAR if n in far else whole(a))
        values.append(a)
    return pl.pallas_call(
        kernel,
        grid=(1,),
        in_specs=specs,
        out_specs=[whole(s) for s in shapes],
        out_shape=[jax.ShapeDtypeStruct(s.shape, s.dtype) for s in shapes],
        scratch_shapes=list(scratch),
        compiler_params=params(),
        cost_estimate=cost(us),
        name=name,
    )(*values)


def body(
    hidden_states,
    entry_rescale_coefficients,
    probe_projection_matrix,
    address_projection_matrix,
    content_projection_matrix,
    final_projection_matrix,
    archive_address_vectors,
    archive_content_vectors,
    reader_sharpness,
    reader_mixing_bias,
    retrieval_assignments,
    document_labels,
):
    rows, piece = hidden_states.shape
    width = probe_projection_matrix.shape[1]
    index = lax.axis_index("mem")
    me = lax.axis_index("tp")
    order = (me + jnp.array([0, -1, 1, 2], jnp.int32)) % 4
    like = jax.ShapeDtypeStruct

    x1 = along_tp(hidden_states, 1)
    x2 = along_tp(hidden_states, -1)
    x3 = along_tp(hidden_states, 2)
    k_own = key_unit(archive_address_vectors)
    (x3,) = ordered(k_own, x3)
    meta = make_meta(retrieval_assignments, index, k_own.shape[0] // MB)
    gain = entry_rescale_coefficients.reshape(4, 1, piece)

    (queries,) = call(
        3,
        query_kernel,
        "norm_query",
        (order,),
        (hidden_states, x1, x2, x3, gain, probe_projection_matrix.reshape(4, piece, width)),
        (like((rows, width), BF16),),
        far=(0, 1, 2, 3, 5),
        scratch=[
            pltpu.VMEM((4, rows, piece), BF16),
            pltpu.VMEM((4, piece, width), BF16),
            pltpu.SemaphoreType.DMA((4,)),
            pltpu.SemaphoreType.DMA((4,)),
        ],
    )

    a1 = first_axis(queries, 1)
    a2 = first_axis(queries, -1)
    a3 = first_axis(queries, 2)
    m1 = jnp.stack([queries, a1])
    m2 = jnp.stack([a2, a3])
    b1p = second_axis(m1, 1)
    b2m = second_axis(m2, -1)
    b1m = second_axis(m1, -1)
    b2p = second_axis(m2, 1)
    x1, x2, x3 = ordered(queries, x1, x2, x3)
    k_own, v_own = ordered(queries, k_own, archive_content_vectors)
    k_sib = other_core(k_own)
    v_sib = other_core(v_own)
    (kv,) = call(
        5,
        kv_kernel,
        "local_kv",
        (order,),
        (
            hidden_states,
            x1,
            x2,
            x3,
            gain,
            address_projection_matrix.reshape(4, piece, width),
            content_projection_matrix.reshape(4, piece, width),
        ),
        (like((2, rows, width), BF16),),
    )
    resident = (k_own, v_own, k_sib, v_sib)
    attend = lambda first, *parts: memory_attention(
        first, meta, reader_sharpness, parts, resident
    )
    m1, m2 = ordered(kv, m1, m2)
    z1, z2 = attend(0, m1, m2)
    b1p, b2m, kv = ordered(z1, b1p, b2m, kv)
    c1 = second_axis(b1p, 1)
    c2 = second_axis(b2m, -1)
    n1, n2, p1, p2 = attend(1, b1p, b2p, b1m, b2m)
    u2 = second_axis(p2, 1)
    v1 = second_axis(n1, -1)
    c1, c2 = ordered(p1, c1, c2)
    f1, f2 = attend(3, c1, c2)

    t1 = second_axis(f1, 1)
    t2 = second_axis(f2, -1)
    count = lax.axis_size("mem")
    before = lax.ppermute(kv, "mem", [(i, i + 1) for i in range(count - 1)])
    kv, queries = ordered(f1, kv, queries)
    (local_out,) = call(
        3,
        local_kernel,
        "local_attention",
        (index[None], reader_sharpness),
        (document_labels.reshape(-1, QB), queries, kv, before),
        (like((rows, width), F32),),
    )
    u1 = second_axis(add(p1, t1), 1)
    v2 = second_axis(add(n2, t2), -1)
    r2 = first_axis(add3(z2[0], u2[0], v2[0]), 1)
    r3 = first_axis(add3(z2[1], u2[1], v2[1]), 2)
    r1 = first_axis(add3(z1[1], u1[1], v1[1]), -1)

    chunk = like((rows // 4, 4 * piece), BF16)
    e0, d1, d2, d3 = call(
        5,
        output_kernel,
        "merge_output",
        (order, reader_mixing_bias),
        ((z1,), (u1,), (v1,), r1, r2, r3, local_out, final_projection_matrix),
        (chunk,) * 4,
        far=(7,),
        scratch=[
            pltpu.VMEM((rows, width), BF16),
            pltpu.VMEM(final_projection_matrix.shape, BF16),
            pltpu.SemaphoreType.DMA,
        ],
    )
    e1 = along_tp(d2, 1)
    e2 = along_tp(d1, -1)
    e3 = along_tp(d3, 2)
    total = e0.astype(F32) + e1.astype(F32) + e2.astype(F32) + e3.astype(F32)
    return total.astype(BF16)


def solution(mesh):
    placed = (
        P("mem", "tp"),
        P(),
        P(None, "tp"),
        P(None, "tp"),
        P(None, "tp"),
        P("tp", None),
        P("mem", "tp"),
        P("mem", "tp"),
        P("tp"),
        P("tp"),
        P(),
        P(),
    )
    return jax.shard_map(
        body, mesh=mesh, in_specs=placed, out_specs=P(("mem", "tp"), None), check_vma=False
    )
```

```python
import functools

import jax
import jax.numpy as jnp
from jax import lax
from jax.experimental import pallas as pl
from jax.experimental.pallas import tpu as pltpu
from jax.sharding import PartitionSpec as P

QB = 128
MB = 512
LOCAL = 256
HD = 128
LOG2E = 1.4426950408889634
NT = (((1,), (1,)), ((), ()))
VMEM = pl.BlockSpec(memory_space=pltpu.VMEM)
SMEM = pl.BlockSpec(memory_space=pltpu.SMEM)
F32 = jnp.float32
BF16 = jnp.bfloat16


def params(mib=24):
    return pltpu.CompilerParams(vmem_limit_bytes=mib * 2**20)


def cost(us):
    return pl.CostEstimate(
        flops=int(us * 1.15e9), bytes_accessed=int(us * 3.69e6), transcendentals=int(us * 1e6)
    )


def unit_into(ref, rows, value):
    for h in range(value.shape[1] // HD):
        part = value[:, h * HD : (h + 1) * HD]
        scale = lax.rsqrt(jnp.mean(part * part, axis=-1, keepdims=True) + 1e-06)
        ref[rows, h * HD : (h + 1) * HD] = (part * scale).astype(BF16)


def norm_pieces(order, pieces, gain):
    pieces = [x[...].astype(F32) for x in pieces]
    total = sum(jnp.sum(p * p, axis=-1, keepdims=True) for p in pieces)
    scale = lax.rsqrt(total / (4 * pieces[0].shape[1]) + 1e-05)
    return [
        (piece * scale * gain[order[p]].astype(F32)).astype(BF16)
        for p, piece in enumerate(pieces)
    ]


def query_kernel(order, x0, x1, x2, x3, gain, weight, queries, x, w, x_sem, w_sem):
    loads = [
        pltpu.make_async_copy(part, x.at[p], x_sem.at[p]) for p, part in enumerate((x0, x1, x2, x3))
    ]
    fetches = [
        pltpu.make_async_copy(weight.at[order[p]], w.at[p], w_sem.at[p]) for p in range(4)
    ]
    for copy in loads + fetches:
        copy.start()
    for copy in loads:
        copy.wait()
    normed = norm_pieces(order, [x.at[p] for p in range(4)], gain)
    result = None
    for p, value in enumerate(normed):
        fetches[p].wait()
        term = jnp.dot(value, w[p], preferred_element_type=F32)
        result = term if result is None else result + term
    unit_into(queries, slice(None), result)


def kv_kernel(order, x0, x1, x2, x3, gain, key_weight, value_weight, kv, w, sem):
    fetches = [
        pltpu.make_async_copy(weight.at[order[p]], w.at[side, p], sem.at[side, p])
        for side, weight in enumerate((key_weight, value_weight))
        for p in range(4)
    ]
    for fetch in fetches:
        fetch.start()
    normed = norm_pieces(order, (x0, x1, x2, x3), gain)
    for side in range(2):
        result = None
        for p, value in enumerate(normed):
            fetches[4 * side + p].wait()
            term = jnp.dot(value, w[side, p], preferred_element_type=F32)
            result = term if result is None else result + term
        if side == 0:
            unit_into(kv.at[0], slice(None), result)
        else:
            kv[1] = result.astype(BF16)


def key_unit_kernel(raw, keys, x, sem):
    blocks = x.shape[0]
    loads = [
        pltpu.make_async_copy(raw.at[pl.ds(b * MB, MB)], x.at[b], sem.at[b]) for b in range(blocks)
    ]
    for load in loads:
        load.start()
    wide = 2 * HD
    place = lambda d: lax.broadcasted_iota(jnp.int32, (wide, wide), d) // HD
    ones = (place(0) == place(1)).astype(BF16)

    def step(b, _):
        pltpu.make_async_copy(raw.at[pl.ds(0, MB)], x.at[b], sem.at[b]).wait()
        rows = pl.ds(pl.multiple_of(b * MB, MB), MB)
        for c in range(x.shape[2] // wide):
            cols = slice(c * wide, (c + 1) * wide)
            part = x[b, :, cols].astype(F32)
            total = jnp.dot((part * part).astype(BF16), ones, preferred_element_type=F32)
            keys[rows, cols] = (part * lax.rsqrt(total * (1 / HD) + 1e-06)).astype(BF16)
        return 0

    lax.fori_loop(0, blocks, step, 0)


def key_unit(raw):
    blocks = raw.shape[0] // MB
    return pl.pallas_call(
        key_unit_kernel,
        in_specs=[pl.BlockSpec(memory_space=pl.ANY)],
        out_specs=VMEM,
        out_shape=jax.ShapeDtypeStruct(raw.shape, BF16),
        scratch_shapes=[
            pltpu.VMEM((blocks, MB, raw.shape[1]), BF16),
            pltpu.SemaphoreType.DMA((blocks,)),
        ],
        compiler_params=params(),
        cost_estimate=cost(30),
        name="key_unit",
    )(raw)


def local_kernel(index, sharp, labels, queries, kv, before, out):
    rows = queries.shape[0]
    place = lax.broadcasted_iota(jnp.int32, (rows, rows), 0)
    other = lax.broadcasted_iota(jnp.int32, (rows, rows), 1)
    line = lambda r: labels[pl.ds(r, 1), :].astype(F32)
    here = 2 * index[0]
    own = [line(here), line(here + 1)]
    past = [line(jnp.maximum(here - 2, 0)), line(jnp.maximum(here - 1, 0))]
    queried = jnp.concatenate(
        [jnp.transpose(jnp.broadcast_to(o, (QB, QB)))[:, :1] for o in own], axis=0
    )
    same_before = (queried == jnp.concatenate(past, axis=1)) & (index[0] > 0)
    same_own = queried == jnp.concatenate(own, axis=1)
    allow_before = (other > place) & same_before
    allow_own = (other <= place) & same_own
    for h in range(queries.shape[1] // HD):
        cols = slice(h * HD, (h + 1) * HD)
        scale = sharp[h] * (LOG2E / HD)
        q = queries[:, cols]
        numer = None
        total = None
        for keep, src in ((allow_before, before), (allow_own, kv)):
            s = lax.dot_general(q, src[0, :, cols], NT, preferred_element_type=F32)
            w = jnp.where(keep, jnp.exp2(s * scale), 0.0)
            t = jnp.sum(w, axis=-1, keepdims=True)
            n = jnp.dot(w.astype(BF16), src[1, :, cols], preferred_element_type=F32)
            numer = n if numer is None else numer + n
            total = t if total is None else total + t
        out[:, cols] = numer / total


def memory_kernel(first, meta, sharp, *refs):
    n = (len(refs) - 8) // 2
    parts, sources = refs[:n], (refs[n : n + 2], refs[n + 2 : n + 4])
    outs, (q, o, in_sem, out_sem) = refs[n + 4 : 2 * n + 4], refs[2 * n + 4 :]
    heads = q.shape[2] // HD
    loads = [
        pltpu.make_async_copy(parts[i // 2].at[i % 2], q.at[i], in_sem.at[i]) for i in range(2 * n)
    ]
    stores = [
        pltpu.make_async_copy(o.at[i], outs[i // 2].at[i % 2], out_sem.at[i]) for i in range(2 * n)
    ]
    for load in loads:
        load.start()
    eye = lax.broadcasted_iota(jnp.int32, (QB, QB), 0) == lax.broadcasted_iota(
        jnp.int32, (QB, QB), 1
    )
    tile_row = lax.broadcasted_iota(jnp.int32, (16, HD), 0)
    cols = [slice(h * HD, (h + 1) * HD) for h in range(heads)]
    o[...] = jnp.zeros_like(o)

    def source(i, _):
        pltpu.make_async_copy(parts[0].at[0], q.at[i], in_sem.at[i]).wait()
        for j, (k, v) in enumerate(sources):
            base = ((first * 4 + i) * 2 + j) * 3

            def slot(j=j, k=k, v=v, base=base):
                half = meta[base + 1]
                rows = pl.ds(pl.multiple_of(half * QB, QB), QB)
                span = pl.ds(pl.multiple_of(meta[base + 2] * MB, MB), MB)
                scores = [
                    lax.dot_general(q[i, rows, c], k[span, c], NT, preferred_element_type=F32)
                    for c in cols
                ]
                weights = [jnp.exp2(s * (sharp[h] * (LOG2E / HD))) for h, s in enumerate(scores)]
                numers = [
                    jnp.dot(w.astype(BF16), v[span, c], preferred_element_type=F32)
                    for w, c in zip(weights, cols)
                ]
                lines = [
                    jnp.sum(
                        jnp.where(eye, jnp.sum(w, axis=-1, keepdims=True), 0.0),
                        axis=0,
                        keepdims=True,
                    )
                    for w in weights
                ]
                for num, line, c in zip(numers, lines, cols):
                    den = jnp.where(tile_row == half, line, 0.0)
                    if j == 1:
                        num = num + o[i, rows, c].astype(F32)
                        den = den + o[i, 2 * QB :, c].astype(F32)
                    o[i, rows, c] = num.astype(BF16)
                    o[i, 2 * QB :, c] = den.astype(BF16)

            pl.when(meta[base] > 0)(slot)
        for t in range(n):
            pl.when(i // 2 == t)(
                lambda t=t: pltpu.make_async_copy(
                    o.at[i], outs[t].at[i - 2 * t], out_sem.at[i]
                ).start()
            )
        return 0

    lax.fori_loop(0, 2 * n, source, 0)
    for store in stores:
        store.wait()


def memory_attention(first, meta, sharp, parts, resident):
    width = parts[0].shape[2]
    n = len(parts)
    shape = jax.ShapeDtypeStruct((2, 2 * QB + 16, width), BF16)
    far = pl.BlockSpec(memory_space=pl.ANY)
    return pl.pallas_call(
        functools.partial(memory_kernel, first),
        in_specs=[SMEM, SMEM] + [far] * n + [VMEM] * 4,
        out_specs=[far] * n,
        out_shape=[shape] * n,
        scratch_shapes=[
            pltpu.VMEM((2 * n, 2 * QB, width), BF16),
            pltpu.VMEM((2 * n, 2 * QB + 16, width), BF16),
            pltpu.SemaphoreType.DMA((2 * n,)),
            pltpu.SemaphoreType.DMA((2 * n,)),
        ],
        compiler_params=params(),
        cost_estimate=cost(15 * n),
        name="memory_attention",
    )(meta, sharp, *parts, *resident)


def output_kernel(
    order, bias, z, u, v, s, x1, x2, x3, local, weight, c0, c1, c2, c3, mixed, w, w_sem
):
    fetch = pltpu.make_async_copy(weight, w, w_sem)
    fetch.start()
    total = z[0].astype(F32) + u[0].astype(F32) + v[0].astype(F32) + s[0].astype(F32)
    total = total + x1[...].astype(F32) + x2[...].astype(F32) + x3[...].astype(F32)
    dens = total[2 * QB :, :]
    for h in range(total.shape[1] // HD):
        cols = slice(h * HD, (h + 1) * HD)
        gate = jax.nn.sigmoid(jnp.full((1, HD), bias[h], F32))
        turned = jnp.transpose(
            jnp.concatenate([dens[:, cols], jnp.zeros((HD - 16, HD), F32)], axis=0)
        )
        for b in range(2):
            rows = slice(b * QB, (b + 1) * QB)
            mem = total[rows, cols] / turned[:, b : b + 1]
            mixed[rows, cols] = (gate * mem + (1.0 - gate) * local[rows, cols]).astype(BF16)
    fetch.wait()
    for j, c in enumerate((c0, c1, c2, c3)):
        n = c.shape[0]
        rows = pl.ds(pl.multiple_of(order[j] * n, n), n)
        c[...] = jnp.dot(mixed[rows, :], w[...], preferred_element_type=F32).astype(c.dtype)


def mem_pairs(move):
    out = []
    for z in range(4):
        for y in range(4):
            for c in range(2):
                tz, ty, tc = move(z, y, c)
                out.append((z * 8 + y * 2 + c, (tz % 4) * 8 + (ty % 4) * 2 + tc))
    return out


def first_axis(value, by):
    pairs = mem_pairs(lambda z, y, c: (z + by, y, c) if c == 0 else (z, y + by, c))
    return lax.ppermute(value, "mem", pairs)


def second_axis(value, by):
    pairs = mem_pairs(lambda z, y, c: (z, y + by, c) if c == 0 else (z + by, y, c))
    return lax.ppermute(value, "mem", pairs)


def other_core(value):
    return lax.ppermute(value, "mem", mem_pairs(lambda z, y, c: (z, y, 1 - c)))


def along_tp(value, by):
    return lax.ppermute(value, "tp", [(i, (i + by) % 4) for i in range(4)])


def make_meta(assign, index, blocks_here):
    z, y, c = index // 8, (index // 2) % 4, index % 2
    shifts = jnp.array([0, -1, 1, 2], jnp.int32)
    second = jnp.array([0, -1, 1, 2], jnp.int32)[:, None]
    first = shifts[None, :]
    sz = jnp.where(c == 0, z + first, z + second) % 4
    sy = jnp.where(c == 0, y + second, y + first) % 4
    source = sz * 8 + sy * 2 + c
    ids = jnp.take(assign.reshape(-1, 16), source.reshape(-1), axis=0)
    holder = jnp.stack([index, index + 1 - 2 * c])
    hit = (ids // blocks_here)[:, None, :] == holder[None, :, None]
    here = jnp.any(hit, axis=-1).astype(jnp.int32).reshape(4, 4, 2)
    block = jnp.sum(jnp.where(hit, (ids % blocks_here)[:, None, :], 0), axis=-1).reshape(4, 4, 2)
    place = jnp.arange(16, dtype=jnp.int32)[None, None, :] // 8
    half = jnp.sum(jnp.where(hit, place, 0), axis=-1).reshape(4, 4, 2)
    return jnp.stack([here, half, block], axis=-1).reshape(-1)


def sum_of(*values):
    return sum(v.astype(F32) for v in values).astype(BF16)


def ordered(first, *later):
    return lax.optimization_barrier((first,) + later)[1:]


FAR = pl.BlockSpec(memory_space=pl.ANY)


def call(us, kernel, name, scalars, arrays, shapes, far=(), scratch=()):
    whole = lambda a: pl.BlockSpec(a.shape, lambda i, n=len(a.shape): (0,) * n)
    specs = [SMEM] * len(scalars)
    values = list(scalars)
    for n, a in enumerate(arrays):
        if isinstance(a, tuple):
            a = a[0]
            specs.append(pl.BlockSpec((1,) + a.shape[1:], lambda i, n=a.ndim: (0,) * n))
        else:
            specs.append(FAR if n in far else whole(a))
        values.append(a)
    return pl.pallas_call(
        kernel,
        grid=(1,),
        in_specs=specs,
        out_specs=[whole(s) for s in shapes],
        out_shape=[jax.ShapeDtypeStruct(s.shape, s.dtype) for s in shapes],
        scratch_shapes=list(scratch),
        compiler_params=params(),
        cost_estimate=cost(5 * us),
        name=name,
    )(*values)


def body(
    hidden_states,
    entry_rescale_coefficients,
    probe_projection_matrix,
    address_projection_matrix,
    content_projection_matrix,
    final_projection_matrix,
    archive_address_vectors,
    archive_content_vectors,
    reader_sharpness,
    reader_mixing_bias,
    retrieval_assignments,
    document_labels,
):
    rows, piece = hidden_states.shape
    width = probe_projection_matrix.shape[1]
    index = lax.axis_index("mem")
    me = lax.axis_index("tp")
    order = (me + jnp.array([0, -1, 1, 2], jnp.int32)) % 4
    like = jax.ShapeDtypeStruct

    x1 = along_tp(hidden_states, 1)
    x2 = along_tp(hidden_states, -1)
    x3 = along_tp(hidden_states, 2)
    k_own = key_unit(archive_address_vectors)
    k_own, v_own = ordered(x1, k_own, archive_content_vectors)
    k_sib = other_core(k_own)
    v_sib = other_core(v_own)
    meta = make_meta(retrieval_assignments, index, k_own.shape[0] // MB)
    gain = entry_rescale_coefficients.reshape(4, 1, piece)
    x3, meta, gain = lax.optimization_barrier((ordered(k_own, x3)[0], meta, gain))

    (queries,) = call(
        3,
        query_kernel,
        "norm_query",
        (order,),
        (hidden_states, x1, x2, x3, gain, probe_projection_matrix.reshape(4, piece, width)),
        (like((rows, width), BF16),),
        far=(0, 1, 2, 3, 5),
        scratch=[
            pltpu.VMEM((4, rows, piece), BF16),
            pltpu.VMEM((4, piece, width), BF16),
            pltpu.SemaphoreType.DMA((4,)),
            pltpu.SemaphoreType.DMA((4,)),
        ],
    )

    a1 = first_axis(queries, 1)
    a2 = first_axis(queries, -1)
    a3 = first_axis(queries, 2)
    x1, x2, x3 = ordered(queries, x1, x2, x3)
    (kv,) = call(
        5,
        kv_kernel,
        "local_kv",
        (order,),
        (
            hidden_states,
            x1,
            x2,
            x3,
            gain,
            address_projection_matrix.reshape(4, piece, width),
            content_projection_matrix.reshape(4, piece, width),
        ),
        (like((2, rows, width), BF16),),
        far=(5, 6),
        scratch=[
            pltpu.VMEM((2, 4, piece, width), BF16),
            pltpu.SemaphoreType.DMA((2, 4)),
        ],
    )
    m1 = jnp.stack([queries, a1])
    a2, a3 = ordered(kv, a2, a3)
    m2 = jnp.stack([a2, a3])
    b1p = second_axis(m1, 1)
    b2m = second_axis(m2, -1)
    b1m = second_axis(m1, -1)
    b2p = second_axis(m2, 1)

    resident = tuple(
        pltpu.with_memory_space_constraint(a, pltpu.VMEM) for a in (k_own, v_own, k_sib, v_sib)
    )
    attend = lambda first, *parts: memory_attention(
        first, meta, reader_sharpness, parts, resident
    )
    z1, z2 = attend(0, m1, m2)
    b1p, b2m, b1m, b2p, kv = ordered(z1, b1p, b2m, b1m, b2p, kv)
    c1 = second_axis(b1p, 1)
    c2 = second_axis(b2m, -1)
    count = lax.axis_size("mem")
    before = lax.ppermute(kv, "mem", [(i, i + 1) for i in range(count - 1)])
    n1, n2, p1, p2 = attend(1, b1p, b2p, b1m, b2m)
    u1 = second_axis(p1, 1)
    u2 = second_axis(p2, 1)
    v1 = second_axis(n1, -1)
    v2 = second_axis(n2, -1)
    c1, c2, before = ordered(p1, c1, c2, before)
    f1, f2 = attend(3, c1, c2)

    s1 = second_axis(f1, 2)
    s2 = second_axis(f2, 2)
    kv, queries, before = ordered(f1, kv, queries, before)
    (local_out,) = call(
        3,
        local_kernel,
        "local_attention",
        (index[None], reader_sharpness),
        (document_labels.reshape(-1, QB), queries, kv, before),
        (like((rows, width), F32),),
    )
    u1, u2, v1, v2, local_out = lax.optimization_barrier((u1, u2, v1, v2, local_out))
    whole = lambda a, i: sum_of(z1[i], u1[i], v1[i], s1[i]) if a == 0 else sum_of(z2[i], u2[i], v2[i], s2[i])
    r3 = first_axis(whole(1, 1), 2)
    r2 = first_axis(whole(1, 0), 1)
    r1 = first_axis(whole(0, 1), -1)

    chunk = like((rows // 4, 4 * piece), BF16)
    e0, d1, d2, d3 = call(
        5,
        output_kernel,
        "merge_output",
        (order, reader_mixing_bias),
        ((z1,), (u1,), (v1,), (s1,), r1, r2, r3, local_out, final_projection_matrix),
        (chunk,) * 4,
        far=(8,),
        scratch=[
            pltpu.VMEM((rows, width), BF16),
            pltpu.VMEM(final_projection_matrix.shape, BF16),
            pltpu.SemaphoreType.DMA,
        ],
    )
    e1 = along_tp(d2, 1)
    e2 = along_tp(d1, -1)
    e3 = along_tp(d3, 2)
    total = e0.astype(F32) + e1.astype(F32) + e2.astype(F32) + e3.astype(F32)
    return total.astype(BF16)


def solution(mesh):
    placed = (
        P("mem", "tp"),
        P(),
        P(None, "tp"),
        P(None, "tp"),
        P(None, "tp"),
        P("tp", None),
        P("mem", "tp"),
        P("mem", "tp"),
        P("tp"),
        P("tp"),
        P(),
        P(),
    )
    return jax.shard_map(
        body, mesh=mesh, in_specs=placed, out_specs=P(("mem", "tp"), None), check_vma=False
    )
```

```python
import functools

import jax
import jax.numpy as jnp
from jax import lax
from jax.experimental import pallas as pl
from jax.experimental.pallas import tpu as pltpu
from jax.sharding import PartitionSpec as P

QB = 128
MB = 512
LOCAL = 256
HD = 128
LOG2E = 1.4426950408889634
NT = (((1,), (1,)), ((), ()))
VMEM = pl.BlockSpec(memory_space=pltpu.VMEM)
SMEM = pl.BlockSpec(memory_space=pltpu.SMEM)
F32 = jnp.float32
BF16 = jnp.bfloat16


def params(mib=24):
    return pltpu.CompilerParams(vmem_limit_bytes=mib * 2**20)


def cost(us):
    return pl.CostEstimate(
        flops=int(us * 1.15e9), bytes_accessed=int(us * 3.69e6), transcendentals=int(us * 1e6)
    )


def unit_into(ref, rows, value):
    for h in range(value.shape[1] // HD):
        part = value[:, h * HD : (h + 1) * HD]
        scale = lax.rsqrt(jnp.mean(part * part, axis=-1, keepdims=True) + 1e-06)
        ref[rows, h * HD : (h + 1) * HD] = (part * scale).astype(BF16)


def norm_pieces(order, pieces, gain):
    pieces = [x[...].astype(F32) for x in pieces]
    total = sum(jnp.sum(p * p, axis=-1, keepdims=True) for p in pieces)
    scale = lax.rsqrt(total / (4 * pieces[0].shape[1]) + 1e-05)
    return [
        (piece * scale * gain[order[p]].astype(F32)).astype(BF16)
        for p, piece in enumerate(pieces)
    ]


def query_kernel(order, x0, x1, x2, x3, gain, weight, queries, x, w, x_sem, w_sem):
    loads = [
        pltpu.make_async_copy(part, x.at[p], x_sem.at[p]) for p, part in enumerate((x0, x1, x2, x3))
    ]
    fetches = [
        pltpu.make_async_copy(weight.at[order[p]], w.at[p], w_sem.at[p]) for p in range(4)
    ]
    for copy in loads + fetches:
        copy.start()
    for copy in loads:
        copy.wait()
    normed = norm_pieces(order, [x.at[p] for p in range(4)], gain)
    result = None
    for p, value in enumerate(normed):
        fetches[p].wait()
        term = jnp.dot(value, w[p], preferred_element_type=F32)
        result = term if result is None else result + term
    unit_into(queries, slice(None), result)


def kv_kernel(order, x0, x1, x2, x3, gain, key_weight, value_weight, kv, w, sem):
    fetches = [
        pltpu.make_async_copy(weight.at[order[p]], w.at[side, p], sem.at[side, p])
        for side, weight in enumerate((key_weight, value_weight))
        for p in range(4)
    ]
    for fetch in fetches:
        fetch.start()
    normed = norm_pieces(order, (x0, x1, x2, x3), gain)
    for side in range(2):
        result = None
        for p, value in enumerate(normed):
            fetches[4 * side + p].wait()
            term = jnp.dot(value, w[side, p], preferred_element_type=F32)
            result = term if result is None else result + term
        if side == 0:
            unit_into(kv.at[0], slice(None), result)
        else:
            kv[1] = result.astype(BF16)


def key_unit_kernel(raw, keys, x, sem):
    blocks = x.shape[0]
    loads = [
        pltpu.make_async_copy(raw.at[pl.ds(b * MB, MB)], x.at[b], sem.at[b]) for b in range(blocks)
    ]
    for load in loads:
        load.start()
    wide = 2 * HD
    place = lambda d: lax.broadcasted_iota(jnp.int32, (wide, wide), d) // HD
    ones = (place(0) == place(1)).astype(BF16)

    def step(b, _):
        pltpu.make_async_copy(raw.at[pl.ds(0, MB)], x.at[b], sem.at[b]).wait()
        rows = pl.ds(pl.multiple_of(b * MB, MB), MB)
        for c in range(x.shape[2] // wide):
            cols = slice(c * wide, (c + 1) * wide)
            part = x[b, :, cols].astype(F32)
            total = jnp.dot((part * part).astype(BF16), ones, preferred_element_type=F32)
            keys[rows, cols] = (part * lax.rsqrt(total * (1 / HD) + 1e-06)).astype(BF16)
        return 0

    lax.fori_loop(0, blocks, step, 0)


def key_unit(raw):
    blocks = raw.shape[0] // MB
    return pl.pallas_call(
        key_unit_kernel,
        in_specs=[pl.BlockSpec(memory_space=pl.ANY)],
        out_specs=VMEM,
        out_shape=jax.ShapeDtypeStruct(raw.shape, BF16),
        scratch_shapes=[
            pltpu.VMEM((blocks, MB, raw.shape[1]), BF16),
            pltpu.SemaphoreType.DMA((blocks,)),
        ],
        compiler_params=params(),
        cost_estimate=cost(30),
        name="key_unit",
    )(raw)


def local_kernel(index, sharp, labels, queries, kv, before, out):
    rows = queries.shape[0]
    place = lax.broadcasted_iota(jnp.int32, (rows, rows), 0)
    other = lax.broadcasted_iota(jnp.int32, (rows, rows), 1)
    line = lambda r: labels[pl.ds(r, 1), :].astype(F32)
    here = 2 * index[0]
    own = [line(here), line(here + 1)]
    past = [line(jnp.maximum(here - 2, 0)), line(jnp.maximum(here - 1, 0))]
    queried = jnp.concatenate(
        [jnp.transpose(jnp.broadcast_to(o, (QB, QB)))[:, :1] for o in own], axis=0
    )
    same_before = (queried == jnp.concatenate(past, axis=1)) & (index[0] > 0)
    same_own = queried == jnp.concatenate(own, axis=1)
    allow_before = (other > place) & same_before
    allow_own = (other <= place) & same_own
    for h in range(queries.shape[1] // HD):
        cols = slice(h * HD, (h + 1) * HD)
        scale = sharp[h] * (LOG2E / HD)
        q = queries[:, cols]
        numer = None
        total = None
        for keep, src in ((allow_before, before), (allow_own, kv)):
            s = lax.dot_general(q, src[0, :, cols], NT, preferred_element_type=F32)
            w = jnp.where(keep, jnp.exp2(s * scale), 0.0)
            t = jnp.sum(w, axis=-1, keepdims=True)
            n = jnp.dot(w.astype(BF16), src[1, :, cols], preferred_element_type=F32)
            numer = n if numer is None else numer + n
            total = t if total is None else total + t
        out[:, cols] = numer / total


def memory_kernel(first, meta, sharp, *refs):
    n = (len(refs) - 8) * 2 // 3
    parts, sources = refs[:n], (refs[n : n + 2], refs[n + 2 : n + 4])
    outs, (q, o, in_sem, out_sem) = refs[n + 4 : -4], refs[-4:]
    heads = q.shape[2] // HD
    loads = [
        pltpu.make_async_copy(parts[i // 2].at[i % 2], q.at[i], in_sem.at[i]) for i in range(2 * n)
    ]
    stores = [
        pltpu.make_async_copy(o.at[i], outs[i // 4].at[i % 4], out_sem.at[i]) for i in range(2 * n)
    ]
    for load in loads:
        load.start()
    eye = lax.broadcasted_iota(jnp.int32, (QB, QB), 0) == lax.broadcasted_iota(
        jnp.int32, (QB, QB), 1
    )
    tile_row = lax.broadcasted_iota(jnp.int32, (16, HD), 0)
    cols = [slice(h * HD, (h + 1) * HD) for h in range(heads)]
    o[...] = jnp.zeros_like(o)

    def source(i, _):
        pltpu.make_async_copy(parts[0].at[0], q.at[i], in_sem.at[i]).wait()
        for j, (k, v) in enumerate(sources):
            base = ((first * 4 + i) * 2 + j) * 3

            def slot(j=j, k=k, v=v, base=base):
                half = meta[base + 1]
                rows = pl.ds(pl.multiple_of(half * QB, QB), QB)
                span = pl.ds(pl.multiple_of(meta[base + 2] * MB, MB), MB)
                scores = [
                    lax.dot_general(q[i, rows, c], k[span, c], NT, preferred_element_type=F32)
                    for c in cols
                ]
                weights = [jnp.exp2(s * (sharp[h] * (LOG2E / HD))) for h, s in enumerate(scores)]
                numers = [
                    jnp.dot(w.astype(BF16), v[span, c], preferred_element_type=F32)
                    for w, c in zip(weights, cols)
                ]
                lines = [
                    jnp.sum(
                        jnp.where(eye, jnp.sum(w, axis=-1, keepdims=True), 0.0),
                        axis=0,
                        keepdims=True,
                    )
                    for w in weights
                ]
                for num, line, c in zip(numers, lines, cols):
                    den = jnp.where(tile_row == half, line, 0.0)
                    if j == 1:
                        num = num + o[i, rows, c].astype(F32)
                        den = den + o[i, 2 * QB :, c].astype(F32)
                    o[i, rows, c] = num.astype(BF16)
                    o[i, 2 * QB :, c] = den.astype(BF16)

            pl.when(meta[base] > 0)(slot)
        for t in range(n // 2):
            pl.when(i // 4 == t)(
                lambda t=t: pltpu.make_async_copy(
                    o.at[i], outs[t].at[i - 4 * t], out_sem.at[i]
                ).start()
            )
        return 0

    lax.fori_loop(0, 2 * n, source, 0)
    for store in stores:
        store.wait()


def memory_attention(first, meta, sharp, parts, resident):
    width = parts[0].shape[2]
    n = len(parts)
    shape = jax.ShapeDtypeStruct((4, 2 * QB + 16, width), BF16)
    far = pl.BlockSpec(memory_space=pl.ANY)
    return pl.pallas_call(
        functools.partial(memory_kernel, first),
        in_specs=[SMEM, SMEM] + [far] * n + [VMEM] * 4,
        out_specs=[far] * (n // 2),
        out_shape=[shape] * (n // 2),
        scratch_shapes=[
            pltpu.VMEM((2 * n, 2 * QB, width), BF16),
            pltpu.VMEM((2 * n, 2 * QB + 16, width), BF16),
            pltpu.SemaphoreType.DMA((2 * n,)),
            pltpu.SemaphoreType.DMA((2 * n,)),
        ],
        compiler_params=params(),
        cost_estimate=cost(15 * n),
        name="memory_attention",
    )(meta, sharp, *parts, *resident)


def output_kernel(
    order, bias, z, u, v, s, x1, x2, x3, local, weight, c0, c1, c2, c3, mixed, w, w_sem
):
    fetch = pltpu.make_async_copy(weight, w, w_sem)
    fetch.start()
    total = z[0].astype(F32) + u[0].astype(F32) + v[0].astype(F32) + s[0].astype(F32)
    total = total + x1[...].astype(F32) + x2[...].astype(F32) + x3[...].astype(F32)
    dens = total[2 * QB :, :]
    for h in range(total.shape[1] // HD):
        cols = slice(h * HD, (h + 1) * HD)
        gate = jax.nn.sigmoid(jnp.full((1, HD), bias[h], F32))
        turned = jnp.transpose(
            jnp.concatenate([dens[:, cols], jnp.zeros((HD - 16, HD), F32)], axis=0)
        )
        for b in range(2):
            rows = slice(b * QB, (b + 1) * QB)
            mem = total[rows, cols] / turned[:, b : b + 1]
            mixed[rows, cols] = (gate * mem + (1.0 - gate) * local[rows, cols]).astype(BF16)
    fetch.wait()
    for j, c in enumerate((c0, c1, c2, c3)):
        n = c.shape[0]
        rows = pl.ds(pl.multiple_of(order[j] * n, n), n)
        c[...] = jnp.dot(mixed[rows, :], w[...], preferred_element_type=F32).astype(c.dtype)


def mem_pairs(move):
    out = []
    for z in range(4):
        for y in range(4):
            for c in range(2):
                tz, ty, tc = move(z, y, c)
                out.append((z * 8 + y * 2 + c, (tz % 4) * 8 + (ty % 4) * 2 + tc))
    return out


def first_axis(value, by):
    pairs = mem_pairs(lambda z, y, c: (z + by, y, c) if c == 0 else (z, y + by, c))
    return lax.ppermute(value, "mem", pairs)


def second_axis(value, by):
    pairs = mem_pairs(lambda z, y, c: (z, y + by, c) if c == 0 else (z + by, y, c))
    return lax.ppermute(value, "mem", pairs)


def other_core(value):
    return lax.ppermute(value, "mem", mem_pairs(lambda z, y, c: (z, y, 1 - c)))


def along_tp(value, by):
    return lax.ppermute(value, "tp", [(i, (i + by) % 4) for i in range(4)])


def make_meta(assign, index, blocks_here):
    z, y, c = index // 8, (index // 2) % 4, index % 2
    shifts = jnp.array([0, -1, 1, 2], jnp.int32)
    second = jnp.array([0, -1, 1, 2], jnp.int32)[:, None]
    first = shifts[None, :]
    sz = jnp.where(c == 0, z + first, z + second) % 4
    sy = jnp.where(c == 0, y + second, y + first) % 4
    source = sz * 8 + sy * 2 + c
    ids = jnp.take(assign.reshape(-1, 16), source.reshape(-1), axis=0)
    holder = jnp.stack([index, index + 1 - 2 * c])
    hit = (ids // blocks_here)[:, None, :] == holder[None, :, None]
    here = jnp.any(hit, axis=-1).astype(jnp.int32).reshape(4, 4, 2)
    block = jnp.sum(jnp.where(hit, (ids % blocks_here)[:, None, :], 0), axis=-1).reshape(4, 4, 2)
    place = jnp.arange(16, dtype=jnp.int32)[None, None, :] // 8
    half = jnp.sum(jnp.where(hit, place, 0), axis=-1).reshape(4, 4, 2)
    return jnp.stack([here, half, block], axis=-1).reshape(-1)


def sum_of(*values):
    return sum(v.astype(F32) for v in values).astype(BF16)


def ordered(first, *later):
    return lax.optimization_barrier((first,) + later)[1:]


FAR = pl.BlockSpec(memory_space=pl.ANY)


def call(us, kernel, name, scalars, arrays, shapes, far=(), scratch=()):
    whole = lambda a: pl.BlockSpec(a.shape, lambda i, n=len(a.shape): (0,) * n)
    specs = [SMEM] * len(scalars)
    values = list(scalars)
    for n, a in enumerate(arrays):
        if isinstance(a, tuple):
            a = a[0]
            specs.append(pl.BlockSpec((1,) + a.shape[1:], lambda i, n=a.ndim: (0,) * n))
        else:
            specs.append(FAR if n in far else whole(a))
        values.append(a)
    return pl.pallas_call(
        kernel,
        grid=(1,),
        in_specs=specs,
        out_specs=[whole(s) for s in shapes],
        out_shape=[jax.ShapeDtypeStruct(s.shape, s.dtype) for s in shapes],
        scratch_shapes=list(scratch),
        compiler_params=params(),
        cost_estimate=cost(5 * us),
        name=name,
    )(*values)


def body(
    hidden_states,
    entry_rescale_coefficients,
    probe_projection_matrix,
    address_projection_matrix,
    content_projection_matrix,
    final_projection_matrix,
    archive_address_vectors,
    archive_content_vectors,
    reader_sharpness,
    reader_mixing_bias,
    retrieval_assignments,
    document_labels,
):
    rows, piece = hidden_states.shape
    width = probe_projection_matrix.shape[1]
    index = lax.axis_index("mem")
    me = lax.axis_index("tp")
    order = (me + jnp.array([0, -1, 1, 2], jnp.int32)) % 4
    like = jax.ShapeDtypeStruct

    x1 = along_tp(hidden_states, 1)
    x2 = along_tp(hidden_states, -1)
    x3 = along_tp(hidden_states, 2)
    k_own = key_unit(archive_address_vectors)
    k_own, v_own = ordered(x1, k_own, archive_content_vectors)
    k_sib = other_core(k_own)
    v_sib = other_core(v_own)
    meta = make_meta(retrieval_assignments, index, k_own.shape[0] // MB)
    gain = entry_rescale_coefficients.reshape(4, 1, piece)
    x3, meta, gain = lax.optimization_barrier((ordered(k_own, x3)[0], meta, gain))

    (queries,) = call(
        3,
        query_kernel,
        "norm_query",
        (order,),
        (hidden_states, x1, x2, x3, gain, probe_projection_matrix.reshape(4, piece, width)),
        (like((rows, width), BF16),),
        far=(0, 1, 2, 3, 5),
        scratch=[
            pltpu.VMEM((4, rows, piece), BF16),
            pltpu.VMEM((4, piece, width), BF16),
            pltpu.SemaphoreType.DMA((4,)),
            pltpu.SemaphoreType.DMA((4,)),
        ],
    )

    a1 = first_axis(queries, 1)
    a2 = first_axis(queries, -1)
    a3 = first_axis(queries, 2)
    x1, x2, x3 = ordered(queries, x1, x2, x3)
    (kv,) = call(
        5,
        kv_kernel,
        "local_kv",
        (order,),
        (
            hidden_states,
            x1,
            x2,
            x3,
            gain,
            address_projection_matrix.reshape(4, piece, width),
            content_projection_matrix.reshape(4, piece, width),
        ),
        (like((2, rows, width), BF16),),
        far=(5, 6),
        scratch=[
            pltpu.VMEM((2, 4, piece, width), BF16),
            pltpu.SemaphoreType.DMA((2, 4)),
        ],
    )
    m1 = jnp.stack([queries, a1])
    a2, a3 = ordered(kv, a2, a3)
    m2 = jnp.stack([a2, a3])
    b1p = second_axis(m1, 1)
    b2m = second_axis(m2, -1)
    b1m = second_axis(m1, -1)
    b2p = second_axis(m2, 1)

    resident = tuple(
        pltpu.with_memory_space_constraint(a, pltpu.VMEM) for a in (k_own, v_own, k_sib, v_sib)
    )
    attend = lambda first, *parts: memory_attention(
        first, meta, reader_sharpness, parts, resident
    )
    (z,) = attend(0, m1, m2)
    b1p, b2m, b1m, b2p, kv = ordered(z, b1p, b2m, b1m, b2p, kv)
    c1 = second_axis(b1p, 1)
    c2 = second_axis(b2m, -1)
    count = lax.axis_size("mem")
    before = lax.ppermute(kv, "mem", [(i, i + 1) for i in range(count - 1)])
    n, p = attend(1, b1p, b2p, b1m, b2m)
    u = second_axis(p, 1)
    v = second_axis(n, -1)
    c1, c2, before = ordered(p, c1, c2, before)
    (f,) = attend(3, c1, c2)

    s = second_axis(f, 2)
    kv, queries, before = ordered(f, kv, queries, before)
    (local_out,) = call(
        3,
        local_kernel,
        "local_attention",
        (index[None], reader_sharpness),
        (document_labels.reshape(-1, QB), queries, kv, before),
        (like((rows, width), F32),),
    )
    u, v, local_out = lax.optimization_barrier((u, v, local_out))
    r3 = first_axis(sum_of(z[3], u[3], v[3], s[3]), 2)
    r2 = first_axis(sum_of(z[2], u[2], v[2], s[2]), 1)
    r1 = first_axis(sum_of(z[1], u[1], v[1], s[1]), -1)

    chunk = like((rows // 4, 4 * piece), BF16)
    e0, d1, d2, d3 = call(
        5,
        output_kernel,
        "merge_output",
        (order, reader_mixing_bias),
        ((z,), (u,), (v,), (s,), r1, r2, r3, local_out, final_projection_matrix),
        (chunk,) * 4,
        far=(8,),
        scratch=[
            pltpu.VMEM((rows, width), BF16),
            pltpu.VMEM(final_projection_matrix.shape, BF16),
            pltpu.SemaphoreType.DMA,
        ],
    )
    e1 = along_tp(d2, 1)
    e2 = along_tp(d1, -1)
    e3 = along_tp(d3, 2)
    total = e0.astype(F32) + e1.astype(F32) + e2.astype(F32) + e3.astype(F32)
    return total.astype(BF16)


def solution(mesh):
    placed = (
        P("mem", "tp"),
        P(),
        P(None, "tp"),
        P(None, "tp"),
        P(None, "tp"),
        P("tp", None),
        P("mem", "tp"),
        P("mem", "tp"),
        P("tp"),
        P("tp"),
        P(),
        P(),
    )
    return jax.shard_map(
        body, mesh=mesh, in_specs=placed, out_specs=P(("mem", "tp"), None), check_vma=False
    )
```
